1024 devices in a mesh: sec: 64 (over z_lo, x), mpo: 16 (over z_hi, y, core).
Axes of the slice: x: 4, y: 4, z: 32 (z_hi: 2, z_lo: 16; z = z_hi * 16 + z_lo), core: 2. Of those that a mesh axis runs over, the one named last changes fastest.
Arguments:
- wavefunction: bfloat16 [256, 256, 256], P('sec'), may hold values from -6 to 6
- left_env: bfloat16 [32, 128, 256, 256], P('mpo', 'sec'), may hold values from -0.1875 to 0.1875
- right_env: bfloat16 [32, 128, 256, 256], P('mpo', 'sec'), may hold values from -0.15625 to 0.15625
- pair_left: int32 [256], P('sec'), may hold values from 0 to 127, as said below
- pair_right: int32 [256], P('sec'), may hold values from 0 to 127, as said below
- mpo_mask: int32 [32, 256], P('mpo', 'sec'), may hold values 0 or 1
Outputs:
- applied: bfloat16 [256, 256, 256], P('sec')
The draws below stay inside these ranges and needn't reach their ends.
Inputs may be any that keep to these rules, and one draw needn't show every extreme that they name: `pair_left`: the left sector of a pair in rows k * 4 to (k + 1) * 4 - 1 lies in sectors k * 2 to (k + 1) * 2 - 1. `pair_right`: the right sector of a pair in rows k * 4 to (k + 1) * 4 - 1 lies in sectors (k - 1) * 2 to (k + 2) * 2 - 1.
All inputs are finite; a program needn't handle non-finite values. No bound on the sum of `mpo_mask` on one device may be relied on, other than what follows from the above.
Results may differ from the reference program's by a relative error of at most 0.005.
Values may be sent and summed in bfloat16 or wider, within the bound.
A program may use at most 32 MiB of HBM per device.

```python
import jax
import jax.numpy as jnp
from jax import lax

B = 256
W = 32
S = 2
P_SIZE = 4
SECTORS = 128
PAIRS = 256


def draw_pair_left(key, part):
    key = jax.random.fold_in(key, 11)
    owner = jnp.arange(PAIRS, dtype=jnp.int32) // P_SIZE
    offset = jax.random.randint(key, (PAIRS,), 0, S, dtype=jnp.int32)
    return owner * S + offset


def draw_pair_right(key, part):
    key = jax.random.fold_in(key, 23)
    key_any, key_low, key_high = jax.random.split(key, 3)
    position = jnp.arange(PAIRS, dtype=jnp.int32)
    owner = position // P_SIZE
    slot = position % P_SIZE
    offset = jax.random.randint(key_any, (PAIRS,), -S, 2 * S, dtype=jnp.int32)
    lower = -1 - jax.random.randint(key_low, (PAIRS,), 0, S, dtype=jnp.int32)
    upper = S + jax.random.randint(key_high, (PAIRS,), 0, S, dtype=jnp.int32)
    offset = jnp.where(slot == 0, lower, jnp.where(slot == P_SIZE - 1, upper, offset))
    return jnp.clip(owner * S + offset, 0, SECTORS - 1)


def place_ends(array, own_key, low, high):
    longest = array.shape.index(max(array.shape))
    spots = []
    for shift in (0, 1):
        where = [jax.random.randint(jax.random.fold_in(own_key, axis), (), 0, length) for axis, length in enumerate(array.shape)]
        where[longest] = (where[longest] + shift) % array.shape[longest]
        spots.append(tuple(where))
    return array.at[spots[0]].set(low).at[spots[1]].set(high)


def block_scale(rng, shape, cuts, smallest, top_value):
    def one(dim, parts):
        draws = jax.random.uniform(jax.random.fold_in(jax.random.fold_in(rng, 6), dim), (parts,), jnp.float32, smallest / len(cuts), top_value / len(cuts))
        return jnp.repeat(jnp.exp(draws), shape[dim] // parts).reshape((-1,) + (1,) * (len(shape) - dim - 1))

    factor_of = one(*cuts[0])
    for cut in cuts[1:]:
        factor_of = factor_of * one(*cut)
    return factor_of


def scatter_about(rng, shape, spread, reach, pieces=(), kind=jnp.bfloat16):
    result = spread * jax.random.normal(rng, shape, jnp.float32)
    if pieces:
        result = result * block_scale(rng, shape, pieces, -0.22, 0.18)
    return jnp.clip(result, -reach, reach).astype(kind)


def setup_inputs(seed: int = 0) -> dict:
    key_list = jax.random.split(jax.random.key(seed), 7)
    wavefunction = scatter_about(key_list[0], (PAIRS, B, B), 1.0, 6.0, ((0, 64),))
    left_env = scatter_about(key_list[1], (W, SECTORS, B, B), (B * 4) ** -0.5, 0.1875, ((0, 16), (1, 64)))
    right_env = scatter_about(key_list[2], (W, SECTORS, B, B), (B * 6) ** -0.5, 0.15625, ((0, 16), (1, 64)))
    pair_left = draw_pair_left(jax.random.fold_in(key_list[6], 71), 0)
    pair_right = draw_pair_right(jax.random.fold_in(key_list[6], 71), 0)
    mpo_mask = place_ends((jax.random.randint(key_list[5], (W, PAIRS), 0, 4) < 3).astype(jnp.int32), jax.random.fold_in(key_list[5], 1), 0, 1)
    return {"wavefunction": wavefunction, "left_env": left_env, "right_env": right_env, "pair_left": pair_left, "pair_right": pair_right, "mpo_mask": mpo_mask}


def reference(wavefunction, left_env, right_env, pair_left, pair_right, mpo_mask):
    def one_pair(index):
        block = wavefunction[index].astype(jnp.float32)
        left_sel = jnp.take(left_env, pair_left[index], axis=1).astype(jnp.float32)
        right_sel = jnp.take(right_env, pair_right[index], axis=1).astype(jnp.float32)
        half = jnp.einsum("wij,jk->wik", left_sel, block).astype(jnp.bfloat16).astype(jnp.float32)
        weights = mpo_mask[:, index].astype(jnp.float32)
        half = half * weights[:, None, None]
        total = jnp.einsum("wik,wlk->il", half, right_sel)
        return total.astype(jnp.bfloat16)

    return lax.map(one_pair, jnp.arange(PAIRS, dtype=jnp.int32))
```

```python
import functools

import jax
import jax.numpy as jnp
from jax import lax
from jax.experimental import pallas as pl
from jax.experimental.pallas import tpu as pltpu
from jax.sharding import PartitionSpec as P

X = 4
CHUNKS = 4
FAR = "z4"
F32, BF16 = jnp.float32, jnp.bfloat16


def kernel(
    n_sec, n_mpo, pairs, left_ix, right_ix, mask,
    psi_hbm, left_hbm, right_hbm, out,
    psi, left, half, part, got, mine, twin, full, *rest,
):
    C = CHUNKS
    G = n_mpo // 2
    z_lo_size = n_sec // X
    ring = 2 * z_lo_size
    wide = rest[:C]
    (in_sem, own_sem, r_send, r_recv, s_send, s_recv, z_send, z_recv, g_send, g_recv, near_sem, far_sem) = rest[C:]
    W, S = left.shape[0], left.shape[1]
    B = psi.shape[-1]
    lc = B // C
    per = 128 // lc
    groups = pairs // per
    rows = B // G

    sec, mpo = lax.axis_index("sec"), lax.axis_index("mpo")
    z_hi, me = mpo // G, mpo % G
    z_lo, x = sec // X, sec % X

    def along_z(step):
        z = lax.rem(z_hi * z_lo_size + z_lo + step + ring, ring)
        return lax.rem(z, z_lo_size) * X + x, (z // z_lo_size) * G + me

    def in_plane(step):
        return sec, z_hi * G + lax.rem(me + step, G)

    has_low, has_high = sec > 0, sec < n_sec - 1
    far = {"z16": (ring // 2,), "z8": (ring // 4, -(ring // 4)), "z4": (ring // 8, -(ring // 8))}[FAR]

    def signal(sem, device):
        pl.semaphore_signal(sem, inc=1, device_id=device, device_id_type=pl.DeviceIdType.MESH)

    def remote(src, dst, send, recv, device):
        return pltpu.make_async_remote_copy(
            src_ref=src, dst_ref=dst, send_sem=send, recv_sem=recv,
            device_id=device, device_id_type=pl.DeviceIdType.MESH,
        )

    barrier = pltpu.get_barrier_semaphore()
    for step in far:
        signal(barrier, along_z(step))
    pl.when(has_low)(lambda: signal(barrier, (sec - 1, mpo)))
    pl.when(has_high)(lambda: signal(barrier, (sec + 1, mpo)))
    for step in range(1, G):
        signal(barrier, in_plane(step))

    loads = [
        pltpu.make_async_copy(left_hbm, left, in_sem.at[0]),
        pltpu.make_async_copy(psi_hbm, psi, in_sem.at[1]),
    ]
    own = [
        pltpu.make_async_copy(right_hbm.at[:, :, pl.ds(c * lc, lc)], wide[c].at[:, pl.ds(S, S)], own_sem.at[c])
        for c in range(C)
    ]
    for copy in loads + own:
        copy.start()

    def to_low(c):
        return remote(right_hbm.at[:, :, pl.ds(c * lc, lc)], wide[c].at[:, pl.ds(2 * S, S)],
                      r_send.at[c, 0], r_recv.at[c, 0], (sec - 1, mpo))

    def to_high(c):
        return remote(right_hbm.at[:, :, pl.ds(c * lc, lc)], wide[c].at[:, pl.ds(0, S)],
                      r_send.at[c, 1], r_recv.at[c, 1], (sec + 1, mpo))

    first = sec * S
    left_at = [jnp.clip(left_ix[p] - first, 0, S - 1) for p in range(pairs)]
    right_at = [jnp.clip(right_ix[p] - first + S, 0, 3 * S - 1) for p in range(pairs)]

    def halves():
        for copy in loads:
            copy.wait()
        for p in range(pairs):
            for w in range(W):
                block = jnp.dot(left[w, left_at[p]], psi[p], preferred_element_type=F32)
                half[w, p] = (block * mask[w, p].astype(F32)).astype(BF16)

    if FAR == "z16":
        halves()
    pl.semaphore_wait(barrier, has_low.astype(jnp.int32) + has_high.astype(jnp.int32) + (G - 1 + len(far)))

    for c in range(C):
        pl.when(has_low)(lambda c=c: to_low(c).start())
        pl.when(has_high)(lambda c=c: to_high(c).start())
    if FAR == "z8":
        signal(far_sem, along_z(-(ring // 4)))
    if FAR == "z4":
        signal(near_sem, along_z(ring // 8))
        signal(near_sem, along_z(-(ring // 8)))
    if FAR != "z16":
        halves()

    sends = []

    def contract(c):
        own[c].wait()
        pl.when(has_high)(lambda: to_low(c).wait_recv())
        pl.when(has_low)(lambda: to_high(c).wait_recv())
        lane = lax.broadcasted_iota(jnp.int32, (B, 128), 1)
        for group in range(groups):
            members = range(group * per, (group + 1) * per)
            sums = [None] * per
            for w in range(W):
                rights = jnp.concatenate([wide[c][w, right_at[p]] for p in members], axis=0)
                for q, p in enumerate(members):
                    term = lax.dot_general(half[w, p], rights, (((1,), (1,)), ((), ())), preferred_element_type=F32)
                    sums[q] = term if sums[q] is None else sums[q] + term
            block = sums[0]
            for q in range(1, per):
                block = jnp.where(lane < q * lc, block, sums[q])
            part[c, :, group] = block.astype(BF16).reshape(G, rows, 128)
        for step in range(1, G):
            copy = remote(part.at[c, lax.rem(me + step, G)], got.at[c, step - 1],
                          s_send.at[c, step - 1], s_recv.at[c, step - 1], in_plane(step))
            copy.start()
            sends.append(copy)

    def twin_copy(c):
        return remote(mine.at[c], twin.at[c], z_send.at[c], z_recv.at[c], along_z(ring // 2))

    def add_up(c):
        total = part[c, me].astype(F32)
        for step in range(1, G):
            remote(part.at[c, 0], got.at[c, step - 1], s_send.at[c, step - 1], s_recv.at[c, step - 1],
                   in_plane(step)).wait_recv()
            total = total + got[c, step - 1].astype(F32)
        mine[c] = total.astype(BF16)
        copy = twin_copy(c)
        copy.start()
        sends.append(copy)

    def hand_back(c):
        twin_copy(c).wait_recv()
        full[c, me] = (mine[c].astype(F32) + twin[c].astype(F32)).astype(BF16)
        for step in range(1, G):
            copy = remote(full.at[c, me], full.at[c, me], g_send.at[c, step - 1], g_recv.at[c, step - 1], in_plane(step))
            copy.start()
            sends.append(copy)

    def place(c):
        for step in range(1, G):
            source = lax.rem(me - step + G, G)
            remote(full.at[c, source], full.at[c, source], g_send.at[c, step - 1], g_recv.at[c, step - 1],
                   in_plane(step)).wait_recv()
        if per == 1:
            for p in range(pairs):
                out[p, :, pl.ds(c * 128, 128)] = full[c, :, p].reshape(B, 128)
        elif c % per == per - 1:
            chunks = range(c - per + 1, c + 1)
            for group in range(groups):
                blocks = [full[k, :, group].reshape(B, 128) for k in chunks]
                for q in range(per):
                    out[group * per + q, :, pl.ds(c // per * 128, 128)] = jnp.concatenate(
                        [b[:, q * lc:(q + 1) * lc] for b in blocks], axis=1
                    )

    for c in range(C):
        contract(c)
        if c == 0 and FAR == "z4":
            pl.semaphore_wait(near_sem, 2)
            signal(far_sem, along_z(-(ring // 4)))
        if c == 1:
            if FAR != "z16":
                pl.semaphore_wait(far_sem, 1)
        if c > 0:
            add_up(c - 1)
    add_up(C - 1)
    for c in range(C):
        hand_back(c)
        if c > 0:
            place(c - 1)
    place(C - 1)

    for c in range(C):
        pl.when(has_low)(lambda c=c: to_low(c).wait_send())
        pl.when(has_high)(lambda c=c: to_high(c).wait_send())
    for copy in sends:
        copy.wait_send()


def per_device(n_sec, n_mpo, wavefunction, left_env, right_env, pair_left, pair_right, mpo_mask):
    pairs, B, _ = wavefunction.shape
    W, S = left_env.shape[:2]
    G = n_mpo // 2
    C = CHUNKS
    lc = B // C
    groups = pairs * lc // 128
    rows = B // G
    piece = (groups, rows, 128)
    smem = pl.BlockSpec(memory_space=pltpu.SMEM)
    hbm = pl.BlockSpec(memory_space=pl.ANY)
    dma = pltpu.SemaphoreType.DMA
    return pl.pallas_call(
        functools.partial(kernel, n_sec, n_mpo, pairs),
        out_shape=jax.ShapeDtypeStruct(wavefunction.shape, BF16),
        in_specs=[smem, smem, smem, hbm, hbm, hbm],
        out_specs=pl.BlockSpec(memory_space=pltpu.VMEM),
        scratch_shapes=[
            pltpu.VMEM((pairs, B, B), BF16),
            pltpu.VMEM((W, S, B, B), BF16),
            pltpu.VMEM((W, pairs, B, B), BF16),
            pltpu.VMEM((C, G) + piece, BF16),
            pltpu.VMEM((C, G - 1) + piece, BF16),
            pltpu.VMEM((C,) + piece, BF16),
            pltpu.VMEM((C,) + piece, BF16),
            pltpu.VMEM((C, G) + piece, BF16),
        ]
        + [pltpu.VMEM((W, 3 * S, lc, B), BF16)] * C
        + [
            dma((2,)), dma((C,)), dma((C, 2)), dma((C, 2)),
            dma((C, G - 1)), dma((C, G - 1)), dma((C,)), dma((C,)),
            dma((C, G - 1)), dma((C, G - 1)),
            pltpu.SemaphoreType.REGULAR, pltpu.SemaphoreType.REGULAR,
        ],
        compiler_params=pltpu.CompilerParams(collective_id=0, has_side_effects=True, vmem_limit_bytes=58 * 2**20),
        cost_estimate=pl.CostEstimate(flops=8 * W * pairs * B**3 // 2, bytes_accessed=8 * pairs * B * B, transcendentals=0),
    )(pair_left, pair_right, mpo_mask, wavefunction, left_env, right_env)


def solution(mesh):
    return jax.shard_map(
        functools.partial(per_device, mesh.shape["sec"], mesh.shape["mpo"]),
        mesh=mesh,
        in_specs=(
            P("sec", None, None),
            P("mpo", "sec", None, None),
            P("mpo", "sec", None, None),
            P("sec"),
            P("sec"),
            P("mpo", "sec"),
        ),
        out_specs=P("sec", None, None),
        check_vma=False,
    )
```

```python
import functools

import jax
import jax.numpy as jnp
from jax import lax
from jax.experimental import pallas as pl
from jax.experimental.pallas import tpu as pltpu
from jax.sharding import PartitionSpec as P

X = 4
CHUNKS = 4
REPLY = 12
LEAD = 2
F32, BF16 = jnp.float32, jnp.bfloat16


def kernel(
    n_sec, n_mpo, pairs, left_ix_hbm, right_ix_hbm, mask_hbm,
    psi_hbm, left_hbm, right_hbm, out,
    left_ix, right_ix, mask, psi, left, half, part, got, mine, twin, full, *rest,
):
    C = CHUNKS
    G = n_mpo // 2
    z_lo_size = n_sec // X
    ring = 2 * z_lo_size
    wide = rest[:C]
    (in_sem, own_sem, r_send, r_recv, s_send, s_recv, z_send, z_recv, g_send, g_recv, far_sem) = rest[C:]
    W, S = left.shape[0], left.shape[1]
    B = psi.shape[-1]
    lc = B // C
    per = 128 // lc
    groups = pairs // per
    rows = B // G

    sec, mpo = lax.axis_index("sec"), lax.axis_index("mpo")
    z_hi, me = mpo // G, mpo % G
    z_lo, x = sec // X, sec % X

    def along_z(step):
        z = lax.rem(z_hi * z_lo_size + z_lo + step + ring, ring)
        return lax.rem(z, z_lo_size) * X + x, (z // z_lo_size) * G + me

    def in_plane(step):
        return sec, z_hi * G + lax.rem(me + step, G)

    has_low, has_high = sec > 0, sec < n_sec - 1

    def signal(sem, device):
        pl.semaphore_signal(sem, inc=1, device_id=device, device_id_type=pl.DeviceIdType.MESH)

    def remote(src, dst, send, recv, device):
        return pltpu.make_async_remote_copy(
            src_ref=src, dst_ref=dst, send_sem=send, recv_sem=recv,
            device_id=device, device_id_type=pl.DeviceIdType.MESH,
        )

    barrier = pltpu.get_barrier_semaphore()
    pl.when(z_hi == 0)(lambda: signal(barrier, along_z(ring // 2)))
    pl.when(has_low)(lambda: signal(barrier, (sec - 1, mpo)))
    pl.when(has_high)(lambda: signal(barrier, (sec + 1, mpo)))
    for step in range(1, G):
        signal(barrier, in_plane(step))

    loads = [
        pltpu.make_async_copy(left_ix_hbm, left_ix, in_sem.at[2]),
        pltpu.make_async_copy(right_ix_hbm, right_ix, in_sem.at[3]),
        pltpu.make_async_copy(mask_hbm, mask, in_sem.at[4]),
        pltpu.make_async_copy(left_hbm, left, in_sem.at[0]),
        pltpu.make_async_copy(psi_hbm, psi, in_sem.at[1]),
    ]
    own = [
        pltpu.make_async_copy(right_hbm.at[:, :, pl.ds(c * lc, lc)], wide[c].at[:, pl.ds(S, S)], own_sem.at[c])
        for c in range(C)
    ]
    for copy in loads + own:
        copy.start()

    def to_low(c):
        return remote(right_hbm.at[:, :, pl.ds(c * lc, lc)], wide[c].at[:, pl.ds(2 * S, S)],
                      r_send.at[c, 0], r_recv.at[c, 0], (sec - 1, mpo))

    def to_high(c):
        return remote(right_hbm.at[:, :, pl.ds(c * lc, lc)], wide[c].at[:, pl.ds(0, S)],
                      r_send.at[c, 1], r_recv.at[c, 1], (sec + 1, mpo))

    def halves():
        for copy in loads:
            copy.wait()
        left_at = [jnp.clip(left_ix[p] - sec * S, 0, S - 1) for p in range(pairs)]
        for p in range(pairs):
            for w in range(W):
                block = jnp.dot(left[w, left_at[p]], psi[p], preferred_element_type=F32)
                half[w, p] = (block * mask[w, p].astype(F32)).astype(BF16)

    pl.semaphore_wait(barrier, has_low.astype(jnp.int32) + has_high.astype(jnp.int32) + z_hi + (G - 1))

    for c in range(C):
        pl.when(has_low)(lambda c=c: to_low(c).start())
        pl.when(has_high)(lambda c=c: to_high(c).start())
    pl.when(z_hi == 1)(lambda: signal(far_sem, along_z(ring // 2)))
    halves()
    first = sec * S
    right_at = [jnp.clip(right_ix[p] - first + S, 0, 3 * S - 1) for p in range(pairs)]

    sends = []

    def contract(c):
        own[c].wait()
        pl.when(has_high)(lambda: to_low(c).wait_recv())
        pl.when(has_low)(lambda: to_high(c).wait_recv())
        lane = lax.broadcasted_iota(jnp.int32, (B, 128), 1)
        for group in range(groups):
            members = range(group * per, (group + 1) * per)
            sums = [None] * per
            for w in range(W):
                rights = jnp.concatenate([wide[c][w, right_at[p]] for p in members], axis=0)
                for q, p in enumerate(members):
                    term = lax.dot_general(half[w, p], rights, (((1,), (1,)), ((), ())), preferred_element_type=F32)
                    sums[q] = term if sums[q] is None else sums[q] + term
            block = sums[0]
            for q in range(1, per):
                block = jnp.where(lane < q * lc, block, sums[q])
            part[c, :, group] = block.astype(BF16).reshape(G, rows, 128)
        for step in range(1, G):
            copy = remote(part.at[c, lax.rem(me + step, G)], got.at[c, step - 1],
                          s_send.at[c, step - 1], s_recv.at[c, step - 1], in_plane(step))
            copy.start()
            sends.append(copy)

    def twin_copy(c):
        return remote(mine.at[c], twin.at[c], z_send.at[c], z_recv.at[c], along_z(ring // 2))

    def add_up(c):
        total = part[c, me].astype(F32)
        for step in range(1, G):
            remote(part.at[c, 0], got.at[c, step - 1], s_send.at[c, step - 1], s_recv.at[c, step - 1],
                   in_plane(step)).wait_recv()
            total = total + got[c, step - 1].astype(F32)
        mine[c] = total.astype(BF16)
        pl.when(z_hi == 1)(lambda: twin_copy(c).start())

    def hand_back(c):
        twin_copy(c).wait_recv()
        for k in range(C):
            if (k < LEAD and c == 0) or (k == c + LEAD - 1 and c > 0):
                pl.when(jnp.logical_and(z_hi == 0, z_lo < REPLY))(lambda k=k: twin_copy(k).start())
        full[c, me] = (mine[c].astype(F32) + twin[c].astype(F32)).astype(BF16)
        for step in range(1, G):
            copy = remote(full.at[c, me], full.at[c, me], g_send.at[c, step - 1], g_recv.at[c, step - 1], in_plane(step))
            copy.start()
            sends.append(copy)

    def place(c):
        for step in range(1, G):
            source = lax.rem(me - step + G, G)
            remote(full.at[c, source], full.at[c, source], g_send.at[c, step - 1], g_recv.at[c, step - 1],
                   in_plane(step)).wait_recv()
        if per == 1:
            for p in range(pairs):
                out[p, :, pl.ds(c * 128, 128)] = full[c, :, p].reshape(B, 128)
        elif c % per == per - 1:
            chunks = range(c - per + 1, c + 1)
            for group in range(groups):
                blocks = [full[k, :, group].reshape(B, 128) for k in chunks]
                for q in range(per):
                    out[group * per + q, :, pl.ds(c // per * 128, 128)] = jnp.concatenate(
                        [b[:, q * lc:(q + 1) * lc] for b in blocks], axis=1
                    )

    for c in range(C):
        contract(c)
        if c > 0:
            add_up(c - 1)
    add_up(C - 1)

    @pl.when(z_hi == 0)
    def _():
        pl.semaphore_wait(far_sem, 1)

        @pl.when(z_lo >= REPLY)
        def _():
            for c in range(C):
                twin_copy(c).start()

    for c in range(C):
        hand_back(c)
        if c > 0:
            place(c - 1)
    place(C - 1)

    for c in range(C):
        pl.when(has_low)(lambda c=c: to_low(c).wait_send())
        pl.when(has_high)(lambda c=c: to_high(c).wait_send())
        twin_copy(c).wait_send()
    for copy in sends:
        copy.wait_send()


def per_device(n_sec, n_mpo, wavefunction, left_env, right_env, pair_left, pair_right, mpo_mask):
    pairs, B, _ = wavefunction.shape
    W, S = left_env.shape[:2]
    G = n_mpo // 2
    C = CHUNKS
    lc = B // C
    groups = pairs * lc // 128
    rows = B // G
    piece = (groups, rows, 128)
    hbm = pl.BlockSpec(memory_space=pl.ANY)
    dma = pltpu.SemaphoreType.DMA
    return pl.pallas_call(
        functools.partial(kernel, n_sec, n_mpo, pairs),
        out_shape=pltpu.VMEM(wavefunction.shape, BF16),
        in_specs=[hbm] * 6,
        out_specs=pl.BlockSpec(memory_space=pltpu.VMEM),
        scratch_shapes=[
            pltpu.SMEM((pairs,), jnp.int32),
            pltpu.SMEM((pairs,), jnp.int32),
            pltpu.SMEM((W, pairs), jnp.int32),
            pltpu.VMEM((pairs, B, B), BF16),
            pltpu.VMEM((W, S, B, B), BF16),
            pltpu.VMEM((W, pairs, B, B), BF16),
            pltpu.VMEM((C, G) + piece, BF16),
            pltpu.VMEM((C, G - 1) + piece, BF16),
            pltpu.VMEM((C,) + piece, BF16),
            pltpu.VMEM((C,) + piece, BF16),
            pltpu.VMEM((C, G) + piece, BF16),
        ]
        + [pltpu.VMEM((W, 3 * S, lc, B), BF16)] * C
        + [
            dma((5,)), dma((C,)), dma((C, 2)), dma((C, 2)),
            dma((C, G - 1)), dma((C, G - 1)), dma((C,)), dma((C,)),
            dma((C, G - 1)), dma((C, G - 1)),
            pltpu.SemaphoreType.REGULAR,
        ],
        compiler_params=pltpu.CompilerParams(collective_id=0, has_side_effects=True, vmem_limit_bytes=58 * 2**20),
        cost_estimate=pl.CostEstimate(flops=8 * W * pairs * B**3 // 2, bytes_accessed=8 * pairs * B * B, transcendentals=0),
    )(pair_left, pair_right, mpo_mask, wavefunction, left_env, right_env)


def solution(mesh):
    return jax.shard_map(
        functools.partial(per_device, mesh.shape["sec"], mesh.shape["mpo"]),
        mesh=mesh,
        in_specs=(
            P("sec", None, None),
            P("mpo", "sec", None, None),
            P("mpo", "sec", None, None),
            P("sec"),
            P("sec"),
            P("mpo", "sec"),
        ),
        out_specs=P("sec", None, None),
        check_vma=False,
    )
```

```python
import functools

import jax
import jax.numpy as jnp
from jax import lax
from jax.experimental import pallas as pl
from jax.experimental.pallas import tpu as pltpu
from jax.sharding import PartitionSpec as P

X = 4
CHUNKS = (64, 64, 64, 64)
REPLY = 8
ANSWER = 1
FLIP = 11
LEAD = 2
F32, BF16 = jnp.float32, jnp.bfloat16


def kernel(
    n_sec, n_mpo, pairs, left_ix_hbm, right_ix_hbm, mask_hbm,
    psi_hbm, left_hbm, right_hbm, out,
    left_ix, right_ix, mask, psi, left, half, part, got, mine, twin, full, *rest,
):
    C = len(CHUNKS)
    G = n_mpo // 2
    z_lo_size = n_sec // X
    ring = 2 * z_lo_size
    wide = rest[:C]
    (in_sem, own_sem, r_send, r_recv, s_send, s_recv, z_send, z_recv, g_send, g_recv, far_sem) = rest[C:]
    W, S = left.shape[0], left.shape[1]
    B = psi.shape[-1]
    start = [sum(CHUNKS[:c]) for c in range(C)]
    per = [128 // n for n in CHUNKS]
    groups = [pairs // n for n in per]
    rows = B // G
    order = sorted(range(1, G), key=lambda step: abs(step - G // 2))

    sec, mpo = lax.axis_index("sec"), lax.axis_index("mpo")
    z_hi, me = mpo // G, mpo % G
    z_lo, x = sec // X, sec % X

    def along_z(step):
        z = lax.rem(z_hi * z_lo_size + z_lo + step + ring, ring)
        return lax.rem(z, z_lo_size) * X + x, (z // z_lo_size) * G + me

    def some(c):
        return pl.ds(0, groups[c])

    def in_plane(step):
        return sec, z_hi * G + lax.rem(me + step, G)

    late = jnp.where(jnp.logical_and(z_lo >= FLIP, x == X - 1), 1 - z_hi, z_hi)
    has_low, has_high = sec > 0, sec < n_sec - 1

    def signal(sem, device):
        pl.semaphore_signal(sem, inc=1, device_id=device, device_id_type=pl.DeviceIdType.MESH)

    def remote(src, dst, send, recv, device):
        return pltpu.make_async_remote_copy(
            src_ref=src, dst_ref=dst, send_sem=send, recv_sem=recv,
            device_id=device, device_id_type=pl.DeviceIdType.MESH,
        )

    barrier = pltpu.get_barrier_semaphore()
    pl.when(has_low)(lambda: signal(barrier, (sec - 1, mpo)))
    pl.when(has_high)(lambda: signal(barrier, (sec + 1, mpo)))
    for step in order:
        signal(barrier, in_plane(step))
    pl.when(late == 0)(lambda: signal(barrier, along_z(ring // 2)))

    loads = [
        pltpu.make_async_copy(left_ix_hbm, left_ix, in_sem.at[2]),
        pltpu.make_async_copy(right_ix_hbm, right_ix, in_sem.at[3]),
        pltpu.make_async_copy(mask_hbm, mask, in_sem.at[4]),
        pltpu.make_async_copy(left_hbm, left, in_sem.at[0]),
        pltpu.make_async_copy(psi_hbm, psi, in_sem.at[1]),
    ]
    own = [
        pltpu.make_async_copy(right_hbm.at[:, :, pl.ds(start[c], CHUNKS[c])], wide[c].at[:, pl.ds(S, S)], own_sem.at[c])
        for c in range(C)
    ]
    for copy in loads + own:
        copy.start()

    def to_low(c):
        return remote(right_hbm.at[:, :, pl.ds(start[c], CHUNKS[c])], wide[c].at[:, pl.ds(2 * S, S)],
                      r_send.at[c, 0], r_recv.at[c, 0], (sec - 1, mpo))

    def to_high(c):
        return remote(right_hbm.at[:, :, pl.ds(start[c], CHUNKS[c])], wide[c].at[:, pl.ds(0, S)],
                      r_send.at[c, 1], r_recv.at[c, 1], (sec + 1, mpo))

    def halves():
        for copy in loads:
            copy.wait()
        left_at = [jnp.clip(left_ix[p] - sec * S, 0, S - 1) for p in range(pairs)]
        for p in range(pairs):
            for w in range(W):
                block = jnp.dot(left[w, left_at[p]], psi[p], preferred_element_type=F32)
                half[w, p] = (block * mask[w, p].astype(F32)).astype(BF16)

    pl.semaphore_wait(barrier, has_low.astype(jnp.int32) + has_high.astype(jnp.int32) + late + (G - 1))

    for c in range(C):
        pl.when(has_low)(lambda c=c: to_low(c).start())
        pl.when(has_high)(lambda c=c: to_high(c).start())
    halves()
    first = sec * S
    right_at = [jnp.clip(right_ix[p] - first + S, 0, 3 * S - 1) for p in range(pairs)]

    sends = []

    def contract(c):
        own[c].wait()
        pl.when(has_high)(lambda: to_low(c).wait_recv())
        pl.when(has_low)(lambda: to_high(c).wait_recv())
        lane = lax.broadcasted_iota(jnp.int32, (B, 128), 1)
        for group in range(groups[c]):
            members = range(group * per[c], (group + 1) * per[c])
            sums = [None] * per[c]
            for w in range(W):
                rights = jnp.concatenate([wide[c][w, right_at[p]] for p in members], axis=0)
                for q, p in enumerate(members):
                    term = lax.dot_general(half[w, p], rights, (((1,), (1,)), ((), ())), preferred_element_type=F32)
                    sums[q] = term if sums[q] is None else sums[q] + term
            block = sums[0]
            for q in range(1, per[c]):
                block = jnp.where(lane < q * CHUNKS[c], block, sums[q])
            part[c, :, group] = block.astype(BF16).reshape(G, rows, 128)
        for step in order:
            copy = remote(part.at[c, lax.rem(me + step, G), some(c)], got.at[c, step - 1, some(c)],
                          s_send.at[c, step - 1], s_recv.at[c, step - 1], in_plane(step))
            copy.start()
            sends.append(copy)

    def twin_copy(c):
        return remote(mine.at[c, some(c)], twin.at[c, some(c)], z_send.at[c], z_recv.at[c], along_z(ring // 2))

    def add_up(c):
        total = part[c, me, some(c)].astype(F32)
        for step in order:
            remote(part.at[c, 0, some(c)], got.at[c, step - 1, some(c)], s_send.at[c, step - 1], s_recv.at[c, step - 1],
                   in_plane(step)).wait_recv()
            total = total + got[c, step - 1, some(c)].astype(F32)
        mine[c, some(c)] = total.astype(BF16)
        pl.when(late == 1)(lambda: twin_copy(c).start())

    def hand_back(c):
        twin_copy(c).wait_recv()
        for k in range(C):
            if (k < LEAD and c == 0) or (k == c + LEAD - 1 and c > 0):
                pl.when(jnp.logical_and(late == 0, z_lo < REPLY))(lambda k=k: twin_copy(k).start())
        full[c, me, some(c)] = (mine[c, some(c)].astype(F32) + twin[c, some(c)].astype(F32)).astype(BF16)
        for step in order:
            copy = remote(full.at[c, me, some(c)], full.at[c, me, some(c)], g_send.at[c, step - 1], g_recv.at[c, step - 1], in_plane(step))
            copy.start()
            sends.append(copy)

    def place(c):
        for step in order:
            source = lax.rem(me - step + G, G)
            remote(full.at[c, source, some(c)], full.at[c, source, some(c)], g_send.at[c, step - 1], g_recv.at[c, step - 1],
                   in_plane(step)).wait_recv()
        last = start[c] + CHUNKS[c]
        if last % 128 == 0:
            chunks = [k for k in range(c + 1) if start[k] >= last - 128]
            for p in range(pairs):
                blocks = [full[k, :, p // per[k]].reshape(B, 128) for k in chunks]
                cuts = [(p % per[k]) * CHUNKS[k] for k in chunks]
                out[p, :, pl.ds(last - 128, 128)] = jnp.concatenate(
                    [b[:, i:i + CHUNKS[k]] for b, i, k in zip(blocks, cuts, chunks)], axis=1
                )

    for c in range(C):
        contract(c)
        if c == ANSWER:
            pl.when(late == 1)(lambda: signal(far_sem, along_z(ring // 2)))
        if c > 0:
            add_up(c - 1)
    add_up(C - 1)

    @pl.when(late == 0)
    def _():
        pl.semaphore_wait(far_sem, 1)

        @pl.when(z_lo >= REPLY)
        def _():
            for c in range(C):
                twin_copy(c).start()

    for c in range(C):
        hand_back(c)
        if c > 0:
            place(c - 1)
    place(C - 1)

    for c in range(C):
        pl.when(has_low)(lambda c=c: to_low(c).wait_send())
        pl.when(has_high)(lambda c=c: to_high(c).wait_send())
        twin_copy(c).wait_send()
    for copy in sends:
        copy.wait_send()


def per_device(n_sec, n_mpo, wavefunction, left_env, right_env, pair_left, pair_right, mpo_mask):
    pairs, B, _ = wavefunction.shape
    W, S = left_env.shape[:2]
    G = n_mpo // 2
    C = len(CHUNKS)
    rows = B // G
    piece = (max(pairs * n // 128 for n in CHUNKS), rows, 128)
    hbm = pl.BlockSpec(memory_space=pl.ANY)
    dma = pltpu.SemaphoreType.DMA
    return pl.pallas_call(
        functools.partial(kernel, n_sec, n_mpo, pairs),
        out_shape=pltpu.VMEM(wavefunction.shape, BF16),
        in_specs=[hbm] * 6,
        out_specs=pl.BlockSpec(memory_space=pltpu.VMEM),
        scratch_shapes=[
            pltpu.SMEM((pairs,), jnp.int32),
            pltpu.SMEM((pairs,), jnp.int32),
            pltpu.SMEM((W, pairs), jnp.int32),
            pltpu.VMEM((pairs, B, B), BF16),
            pltpu.VMEM((W, S, B, B), BF16),
            pltpu.VMEM((W, pairs, B, B), BF16),
            pltpu.VMEM((C, G) + piece, BF16),
            pltpu.VMEM((C, G - 1) + piece, BF16),
            pltpu.VMEM((C,) + piece, BF16),
            pltpu.VMEM((C,) + piece, BF16),
            pltpu.VMEM((C, G) + piece, BF16),
        ]
        + [pltpu.VMEM((W, 3 * S, n, B), BF16) for n in CHUNKS]
        + [
            dma((5,)), dma((C,)), dma((C, 2)), dma((C, 2)),
            dma((C, G - 1)), dma((C, G - 1)), dma((C,)), dma((C,)),
            dma((C, G - 1)), dma((C, G - 1)),
            pltpu.SemaphoreType.REGULAR,
        ],
        compiler_params=pltpu.CompilerParams(collective_id=0, has_side_effects=True, vmem_limit_bytes=58 * 2**20),
        cost_estimate=pl.CostEstimate(flops=8 * W * pairs * B**3 // 2, bytes_accessed=8 * pairs * B * B, transcendentals=0),
    )(pair_left, pair_right, mpo_mask, wavefunction, left_env, right_env)


def solution(mesh):
    return jax.shard_map(
        functools.partial(per_device, mesh.shape["sec"], mesh.shape["mpo"]),
        mesh=mesh,
        in_specs=(
            P("sec", None, None),
            P("mpo", "sec", None, None),
            P("mpo", "sec", None, None),
            P("sec"),
            P("sec"),
            P("mpo", "sec"),
        ),
        out_specs=P("sec", None, None),
        check_vma=False,
    )
```
